32 devices in a mesh: occ: 4 (over x, core), vir: 8 (over z, y).
Axes of the slice: x: 2, y: 2, z: 4, core: 2. Of those that a mesh axis runs over, the one named last changes fastest.
Arguments:
- amplitudes: bfloat16 [4, 2, 4096, 4096], P('occ', None, None, 'vir'), may hold values from -6 to 6
- coulomb: bfloat16 [4, 2, 4096, 4096], P('occ', None, None, 'vir'), may hold values from -6 to 6
- ladder_tiles: bfloat16 [256, 128, 128], P('vir'), may hold values from -0.1875 to 0.1875
- cycle_tiles: bfloat16 [256, 128, 128], P('vir'), may hold values from -0.25 to 0.25
- ladder_screen: int32 [32, 8], replicated, may hold values from 0 to 31, as said below
- tile_slot: int32 [256], replicated, may hold values from 0 to 255, each once
- cycle_screen: int32 [64, 4], replicated, may hold values from 0 to 63, as said below
- cycle_rows: int32 [32, 48], replicated, may hold values from 0 to 63, as said below
- cycle_count: int32 [32], replicated, may hold values from 1 to 48, 1024 in all
- slab_occ: int32 [4], replicated, may hold values from 0 to 399
- window_occ: int32 [2], replicated, may hold values from 0 to 399
- occ_energy: float32 [400], replicated, may hold values from -3 to -0.5
- vir_energy: float32 [4096], replicated, may hold values from 0.4 to 4
Outputs:
- updated: bfloat16 [4, 2, 4096, 4096], P('occ', None, None, 'vir')
The draws below stay inside these ranges and needn't reach their ends.
Inputs may be any that keep to these rules, and one draw needn't show every extreme that they name: `ladder_screen`: each row names 8 different tiles. `cycle_screen`: each row names 4 different row tiles. `cycle_rows`: each row names 48 different block columns; the first cycle_count of them are used. `cycle_count`: the counts sum to exactly 1024, and the largest is exactly 48.
All inputs are finite; a program needn't handle non-finite values.
Results may differ from the reference program's by a relative error of at most 0.003.
Values may be sent and summed in bfloat16 or wider, within the bound.
A program may use at most 192 MiB of HBM per device.

```python
import math
import jax
import jax.numpy as jnp
import numpy as np
from jax import lax

VIRT = 4096
TILE = 128
NOCC = 400
OJ = 2
KL = 8
KZ = 4
RMOST = 48
RTOTAL = 1024
NVT = 32
OI = 4


def distinct_rows(key, count, span, keep):
    keys = jax.random.split(key, count)
    return jax.vmap(lambda single: jax.random.permutation(single, span)[:keep])(keys).astype(jnp.int32)


def draw_ladder_screen(key, part):
    return distinct_rows(jax.random.fold_in(key, 11), NVT, NVT, KL)


def draw_cycle_screen(key, part):
    return distinct_rows(jax.random.fold_in(key, 23), OJ * NVT, OJ * NVT, KZ)


def draw_cycle_rows(key, part):
    return distinct_rows(jax.random.fold_in(key, 37), NVT, OJ * NVT, RMOST)


def set_ends(drawn, key, smallest, largest):
    spot = [jax.random.randint(jax.random.fold_in(key, axis), (), 0, length) for axis, length in enumerate(drawn.shape)]
    longest = drawn.shape.index(max(drawn.shape))
    beside = spot[:longest] + [(spot[longest] + 1) % drawn.shape[longest]] + spot[longest + 1:]
    return drawn.at[tuple(spot)].set(smallest).at[tuple(beside)].set(largest)


def levels(rng, dims, cuts, smallest, top_value):
    level, own = 1.0, jax.random.fold_in(rng, 6)
    for dim, parts in cuts:
        steps = jnp.exp(jax.random.uniform(jax.random.fold_in(own, dim), (parts,), jnp.float32, smallest / len(cuts), top_value / len(cuts)))
        level = level * jnp.repeat(steps, dims[dim] // parts).reshape([-1 if axis == dim else 1 for axis in range(len(dims))])
    return level


def length_profile(count, total, bound, lean):
    portions = [(1 << 20) // math.isqrt(grade ** lean) + 1 for grade in range(2, count + 1)]
    spare, given = total - bound - (count - 1), [1] * (count - 1)
    while spare > 0:
        movable = [i for i in range(count - 1) if given[i] < bound]
        mass, budget = sum([portions[i] for i in movable]), spare
        for i in movable:
            more = min(bound - given[i], max(1, budget * portions[i] // mass), spare)
            given[i] = given[i] + more
            spare = spare - more
    return np.array([bound] + given)


def ragged_sizes(rng, count, total, most, skew):
    if count == 2:
        one = jax.random.randint(rng, (), max(1, total - most), min(most, total - 1) + 1)
        return jnp.stack([one, total - one])
    sizes = jnp.asarray(length_profile(count, total, most, skew), jnp.int32)
    twos = (count - 1) // 2
    giver, receiver = sizes[1:1 + 2 * twos:2], sizes[2:2 + 2 * twos:2]
    slack = jnp.minimum(giver - 1, most - receiver)
    passed = jax.random.randint(jax.random.fold_in(rng, 1), (twos,), 0, 1 << 20) % (slack + 1)
    sizes = sizes.at[1:1 + 2 * twos:2].set(giver - passed).at[2:2 + 2 * twos:2].set(receiver + passed)
    return sizes[jax.random.permutation(jax.random.fold_in(rng, 2), count)]


def centred(key, extent, deviation, most, cuts=(), held_as=jnp.bfloat16):
    array = jax.random.normal(key, extent, jnp.float32) * deviation
    if len(cuts) > 0:
        array = levels(key, extent, cuts, -0.22, 0.18) * array
    return jnp.clip(array, min=-most, max=most).astype(held_as)


def setup_inputs(seed: int = 0) -> dict:
    seeds = jax.random.split(jax.random.key(seed), 14)
    return {
        "amplitudes": centred(seeds[0], (OI, OJ, VIRT, VIRT), 1.0, 6.0, ((0, 4), (3, 8))),
        "coulomb": centred(seeds[1], (OI, OJ, VIRT, VIRT), 1.0, 6.0, ((0, 4), (3, 8))),
        "ladder_tiles": centred(seeds[2], (NVT * KL, TILE, TILE), (TILE * KL) ** -0.5, 0.1875, ((0, 8),)),
        "cycle_tiles": centred(seeds[3], (OJ * NVT * KZ, TILE, TILE), (TILE * KZ) ** -0.5, 0.25, ((0, 8),)),
        "ladder_screen": draw_ladder_screen(jax.random.fold_in(seeds[13], 71), 0),
        "tile_slot": jax.random.permutation(seeds[5], NVT * KL).astype(jnp.int32),
        "cycle_screen": draw_cycle_screen(jax.random.fold_in(seeds[13], 71), 0),
        "cycle_rows": draw_cycle_rows(jax.random.fold_in(seeds[13], 71), 0),
        "cycle_count": ragged_sizes(seeds[8], NVT, RTOTAL, RMOST, 2).astype(jnp.int32),
        "slab_occ": set_ends(jax.random.randint(seeds[9], (OI,), 0, NOCC), jax.random.fold_in(seeds[9], 1), 0, NOCC - 1).astype(jnp.int32),
        "window_occ": jax.random.randint(seeds[10], (OJ,), 0, NOCC).astype(jnp.int32),
        "occ_energy": jnp.clip(jax.random.uniform(seeds[11], (NOCC,), jnp.float32, -3.0, -0.5), -3.0, -0.5),
        "vir_energy": jnp.clip(jnp.exp(jax.random.uniform(seeds[12], (VIRT,), jnp.float32, math.log(0.4), math.log(4.0))), 0.4, 4.0),
    }


def reference(amplitudes, coulomb, ladder_tiles, cycle_tiles, ladder_screen, tile_slot, cycle_screen, cycle_rows, cycle_count, slab_occ, window_occ, occ_energy, vir_energy):
    chosen = ladder_tiles[tile_slot.reshape(NVT, KL)]
    cycle_sel = cycle_tiles.reshape(OJ * NVT, KZ, TILE, TILE)
    ends = jnp.cumsum(cycle_count).astype(jnp.int32)
    entry = jnp.arange(RTOTAL, dtype=jnp.int32)
    owner = jnp.sum((ends[None, :] <= entry[:, None]).astype(jnp.int32), axis=1).astype(jnp.int32)
    place = (entry - ends[owner] + cycle_count[owner]).astype(jnp.int32)
    columns = cycle_rows[owner, place]
    energy_j = occ_energy[window_occ]

    def one_row(index):
        amp = lax.dynamic_index_in_dim(amplitudes, index, 0, keepdims=False)
        near = lax.dynamic_index_in_dim(coulomb, index, 0, keepdims=False)
        arranged = amp.transpose(1, 0, 2).reshape(NVT, TILE, OJ * VIRT)
        total = jnp.zeros((NVT, TILE, OJ * VIRT), jnp.float32)
        for level in range(KL):
            total = total + jnp.einsum('arc,ace->are', chosen[:, level].astype(jnp.float32), arranged[ladder_screen[:, level]].astype(jnp.float32))
        ladder = total.reshape(VIRT, OJ, VIRT).transpose(1, 0, 2)
        tiles = amp.reshape(OJ, NVT, TILE, NVT, TILE).transpose(0, 3, 1, 2, 4).reshape(OJ * NVT, NVT, TILE, TILE)
        part = jnp.zeros((RTOTAL, TILE, TILE), jnp.float32)
        for level in range(KZ):
            picked = tiles[cycle_screen[columns, level], owner]
            part = part + jnp.einsum('erc,ecb->erb', picked.astype(jnp.float32), cycle_sel[columns, level].astype(jnp.float32))
        cycle = jnp.zeros((OJ * NVT, NVT, TILE, TILE), jnp.float32).at[columns, owner].add(part).astype(jnp.bfloat16)
        cycle = cycle.reshape(OJ, NVT, NVT, TILE, TILE).transpose(0, 2, 3, 1, 4).reshape(OJ, VIRT, VIRT)
        energy_i = occ_energy[slab_occ[index]]
        denominator = vir_energy[None, :, None] + vir_energy[None, None, :] - energy_i - energy_j[:, None, None]
        value = near.astype(jnp.float32) + ladder + cycle.astype(jnp.float32)
        return (value / denominator).astype(jnp.bfloat16)

    return lax.map(one_row, jnp.arange(OI, dtype=jnp.int32))
```

```python
import functools

import jax
import jax.numpy as jnp
from jax import lax
from jax.experimental import pallas as pl
from jax.experimental.pallas import tpu as pltpu
from jax.sharding import PartitionSpec as P

MESH = pl.DeviceIdType.MESH
VMEM_BYTES = 56 * 1024 * 1024


def bits_down(count):
    bits, bit = [], count // 2
    while bit >= 1:
        bits.append(bit)
        bit //= 2
    return bits


def flipped(index, bit):
    return index + bit - 2 * bit * ((index // bit) % 2)


def spread_order(count):
    return sorted(range(1, count), key=lambda step: abs(step - count // 2))


def send_kernel(occ_count, vir_count, t_ref, w_ref, z_ref, tx_ref, wall_ref, zall_ref,
                own_sem, t_send, t_recv, g_send, g_recv):
    occ, vir = lax.axis_index("occ"), lax.axis_index("vir")
    rows = tx_ref.shape[2]
    sub = wall_ref.shape[2]
    occ_bits, vir_bits = bits_down(occ_count), bits_down(vir_count)

    barrier = pltpu.get_barrier_semaphore()
    for step in range(1, vir_count):
        peer = (vir + step) % vir_count
        pl.semaphore_signal(barrier, inc=1, device_id=(occ, peer), device_id_type=MESH)
    for bit in occ_bits:
        pl.semaphore_signal(barrier, inc=1, device_id=(flipped(occ, bit), vir), device_id_type=MESH)
    pl.semaphore_wait(barrier, vir_count - 1 + len(occ_bits))

    own = []
    for place, (src, dst) in enumerate(((w_ref, wall_ref), (z_ref, zall_ref))):
        copy = pltpu.make_async_copy(src.at[pl.ds(occ * sub, sub)], dst.at[vir, occ], own_sem.at[place])
        copy.start()
        own.append(copy)
    keep = pltpu.make_async_copy(t_ref.at[0, :, pl.ds(vir * rows, rows), :], tx_ref.at[vir], own_sem.at[2])
    keep.start()
    for copy in own:
        copy.wait()

    count = 0

    def exchange(views, device_id):
        nonlocal count
        copies = []
        for view in views:
            for ref in (zall_ref, wall_ref):
                copy = pltpu.make_async_remote_copy(
                    src_ref=view(ref), dst_ref=view(ref), send_sem=g_send.at[count], recv_sem=g_recv.at[count],
                    device_id=device_id, device_id_type=MESH)
                copy.start()
                copies.append(copy)
                count += 1
        return copies

    bit = vir_bits[0]
    pending = exchange([lambda ref: ref.at[vir, occ]], (occ, flipped(vir, bit)))
    held = [vir, flipped(vir, bit)]

    moves = []
    for place, step in enumerate(spread_order(vir_count)):
        peer = (vir + step) % vir_count
        copy = pltpu.make_async_remote_copy(
            src_ref=t_ref.at[0, :, pl.ds(peer * rows, rows), :], dst_ref=tx_ref.at[vir],
            send_sem=t_send.at[place], recv_sem=t_recv.at[place],
            device_id=(occ, peer), device_id_type=MESH)
        copy.start()
        moves.append(copy)

    for copy in pending:
        copy.wait()
    for bit in vir_bits[1:]:
        pending = exchange([functools.partial(lambda at, ref: ref.at[at, occ], at) for at in held],
                           (occ, flipped(vir, bit)))
        for copy in pending:
            copy.wait()
        held = held + [flipped(at, bit) for at in held]
    held = [occ]
    for bit in occ_bits:
        pending = exchange([functools.partial(lambda at, ref: ref.at[:, at], at) for at in held],
                           (flipped(occ, bit), vir))
        for copy in pending:
            copy.wait()
        held = held + [flipped(at, bit) for at in held]
    keep.wait()
    for copy in moves:
        copy.wait()


def send_tiles(amplitudes, ladder_tiles, cycle_tiles, occ_count, vir_count):
    slab_rows, window, width_all, block_cols = amplitudes.shape
    stored, side, _ = ladder_tiles.shape
    rows, sub = width_all // vir_count, stored // occ_count
    gathers = 2 * (vir_count - 1 + occ_count - 1)
    every = jax.ShapeDtypeStruct((vir_count, occ_count, sub, side, side), jnp.bfloat16)
    return pl.pallas_call(
        functools.partial(send_kernel, occ_count, vir_count),
        out_shape=(jax.ShapeDtypeStruct((vir_count, window, rows, block_cols), jnp.bfloat16), every, every),
        in_specs=[pl.BlockSpec(memory_space=pl.ANY)] * 3,
        out_specs=(pl.BlockSpec(memory_space=pl.ANY),) * 3,
        scratch_shapes=[
            pltpu.SemaphoreType.DMA((3,)),
            pltpu.SemaphoreType.DMA((vir_count - 1,)),
            pltpu.SemaphoreType.DMA((vir_count - 1,)),
            pltpu.SemaphoreType.DMA((gathers,)),
            pltpu.SemaphoreType.DMA((gathers,)),
        ],
        compiler_params=pltpu.CompilerParams(
            collective_id=0, has_side_effects=True, vmem_limit_bytes=VMEM_BYTES),
    )(amplitudes, ladder_tiles, cycle_tiles)


def cycle_kernel(screen_ref, used_ref, tx_ref, z_ref, out_ref):
    vir_count, window, rows, block_cols = tx_ref.shape
    side = z_ref.shape[1]
    here, tiles_here = block_cols // side, rows // side
    keep = screen_ref.shape[1]
    tile_count = screen_ref.shape[0] // window
    dest = pl.program_id(0)
    for j in range(window):
        for col in range(here):
            q = j * tile_count + dest * here + col
            picked, weights = [], []
            for m in range(keep):
                u = screen_ref[q, m]
                k, tile = u // tile_count, u % tile_count
                lanes = pl.ds(pl.multiple_of((tile % here) * side, side), side)
                picked.append(tx_ref[tile // here, k, :, lanes])
                weights.append(z_ref[q * keep + m])
            part = jnp.dot(
                jnp.concatenate(picked, axis=1), jnp.concatenate(weights, axis=0),
                preferred_element_type=jnp.float32)
            for a in range(tiles_here):
                span = slice(a * side, (a + 1) * side)
                kept = jnp.where(used_ref[a, q] > 0, part[span], 0.0)
                out_ref[0, j, span, col * side:(col + 1) * side] = kept.astype(jnp.bfloat16)


def cycle_term(cycle_screen, used, moved, all_cycle):
    vir_count, window, rows, block_cols = moved.shape
    return pl.pallas_call(
        cycle_kernel,
        out_shape=jax.ShapeDtypeStruct(moved.shape, jnp.bfloat16),
        grid=(vir_count,),
        in_specs=[
            pl.BlockSpec(memory_space=pltpu.SMEM),
            pl.BlockSpec(memory_space=pltpu.SMEM),
            pl.BlockSpec(moved.shape, lambda d: (0, 0, 0, 0)),
            pl.BlockSpec(all_cycle.shape, lambda d: (0, 0, 0)),
        ],
        out_specs=pl.BlockSpec((1, window, rows, block_cols), lambda d: (d, 0, 0, 0)),
        compiler_params=pltpu.CompilerParams(vmem_limit_bytes=VMEM_BYTES),
    )(cycle_screen, used, moved, all_cycle)


def back_kernel(vir_count, part_ref, out_ref, own_sem, send_sem, recv_sem):
    occ, vir = lax.axis_index("occ"), lax.axis_index("vir")
    rows = part_ref.shape[2]
    barrier = pltpu.get_barrier_semaphore()
    for step in range(1, vir_count):
        peer = (vir + step) % vir_count
        pl.semaphore_signal(barrier, inc=1, device_id=(occ, peer), device_id_type=MESH)
    pl.semaphore_wait(barrier, vir_count - 1)
    place_here = out_ref.at[:, pl.ds(vir * rows, rows), :]
    moves = []
    for place, step in enumerate(spread_order(vir_count)):
        peer = (vir + step) % vir_count
        copy = pltpu.make_async_remote_copy(
            src_ref=part_ref.at[peer], dst_ref=place_here,
            send_sem=send_sem.at[place], recv_sem=recv_sem.at[place],
            device_id=(occ, peer), device_id_type=MESH)
        copy.start()
        moves.append(copy)
    keep = pltpu.make_async_copy(part_ref.at[vir], place_here, own_sem)
    keep.start()
    keep.wait()
    for copy in moves:
        copy.wait()


def send_back(part, vir_count):
    _, window, rows, block_cols = part.shape
    return pl.pallas_call(
        functools.partial(back_kernel, vir_count),
        out_shape=jax.ShapeDtypeStruct((window, vir_count * rows, block_cols), jnp.bfloat16),
        in_specs=[pl.BlockSpec(memory_space=pl.ANY)],
        out_specs=pl.BlockSpec(memory_space=pl.ANY),
        scratch_shapes=[
            pltpu.SemaphoreType.DMA,
            pltpu.SemaphoreType.DMA((vir_count - 1,)),
            pltpu.SemaphoreType.DMA((vir_count - 1,)),
        ],
        compiler_params=pltpu.CompilerParams(
            collective_id=1, has_side_effects=True, vmem_limit_bytes=VMEM_BYTES),
    )(part)


def update_kernel(screen_ref, slot_ref, energy_ref, t_ref, w_ref, row_ref, col_ref, near_ref, cycle_ref, out_ref):
    window = t_ref.shape[1]
    keep = screen_ref.shape[1]
    a = pl.program_id(0)
    weights = jnp.concatenate([w_ref[slot_ref[a * keep + k]] for k in range(keep)], axis=1)
    sums = row_ref[...] + col_ref[...] - energy_ref[0]
    for j in range(window):
        picked = jnp.concatenate([t_ref[0, j, screen_ref[a, k]] for k in range(keep)], axis=0)
        ladder = jnp.dot(weights, picked, preferred_element_type=jnp.float32)
        value = near_ref[0, j].astype(jnp.float32) + ladder + cycle_ref[j].astype(jnp.float32)
        out_ref[0, j] = (value / (sums - energy_ref[1 + j])).astype(jnp.bfloat16)


def update(ladder_screen, tile_slot, energies, amplitudes, all_ladder, energy_a, energy_b, coulomb, cycle):
    _, window, width_all, block_cols = amplitudes.shape
    side = all_ladder.shape[1]
    tile_count = width_all // side
    tiled = amplitudes.reshape(1, window, tile_count, side, block_cols)
    block = pl.BlockSpec((1, window, side, block_cols), lambda a: (0, 0, a, 0))
    smem = pl.BlockSpec(memory_space=pltpu.SMEM)
    return pl.pallas_call(
        update_kernel,
        out_shape=jax.ShapeDtypeStruct(amplitudes.shape, jnp.bfloat16),
        grid=(tile_count,),
        in_specs=[
            smem, smem, smem,
            pl.BlockSpec(tiled.shape, lambda a: (0, 0, 0, 0, 0)),
            pl.BlockSpec(all_ladder.shape, lambda a: (0, 0, 0)),
            pl.BlockSpec((side, 1), lambda a: (a, 0)),
            pl.BlockSpec((1, block_cols), lambda a: (0, 0)),
            block,
            pl.BlockSpec((window, side, block_cols), lambda a: (0, a, 0)),
        ],
        out_specs=block,
        compiler_params=pltpu.CompilerParams(vmem_limit_bytes=VMEM_BYTES),
    )(ladder_screen, tile_slot, energies, tiled, all_ladder, energy_a, energy_b, coulomb, cycle)


def body(
    amplitudes, coulomb, ladder_tiles, cycle_tiles, ladder_screen, tile_slot, cycle_screen,
    cycle_rows, cycle_count, slab_occ, window_occ, occ_energy, vir_energy,
):
    occ_count, vir_count = lax.axis_size("occ"), lax.axis_size("vir")
    slab_rows, window, width_all, block_cols = amplitudes.shape
    stored, side, _ = ladder_tiles.shape
    tile_count = width_all // side
    tiles_here = tile_count // vir_count
    occ, vir = lax.axis_index("occ"), lax.axis_index("vir")

    columns = lax.dynamic_slice_in_dim(cycle_rows, vir * tiles_here, tiles_here, 0)
    counts = lax.dynamic_slice_in_dim(cycle_count, vir * tiles_here, tiles_here, 0)
    listed = jnp.arange(columns.shape[1], dtype=jnp.int32)[None, :] < counts[:, None]
    every_q = jnp.arange(cycle_screen.shape[0], dtype=jnp.int32)
    used = jnp.any((columns[:, :, None] == every_q[None, None, :]) & listed[:, :, None], axis=1).astype(jnp.int32)

    orbital_ids = jnp.arange(occ_energy.shape[0], dtype=jnp.int32)
    wanted = jnp.concatenate([lax.dynamic_slice_in_dim(slab_occ, occ * slab_rows, slab_rows), window_occ])
    energies = jnp.sum(jnp.where(wanted[:, None] == orbital_ids[None, :], occ_energy[None, :], 0.0), axis=1)
    energy_a = vir_energy.reshape(width_all, 1)
    energy_b = lax.dynamic_slice_in_dim(vir_energy, vir * block_cols, block_cols).reshape(1, block_cols)

    moved, all_ladder, all_cycle = send_tiles(amplitudes, ladder_tiles, cycle_tiles, occ_count, vir_count)
    all_ladder = all_ladder.reshape(vir_count * stored, side, side)
    all_cycle = all_cycle.reshape(vir_count * stored, side, side)
    part = cycle_term(cycle_screen, used, moved, all_cycle)
    cycle = send_back(part, vir_count)
    return update(ladder_screen, tile_slot, energies, amplitudes, all_ladder, energy_a, energy_b, coulomb, cycle)


def solution(mesh):
    return jax.shard_map(
        body,
        mesh=mesh,
        in_specs=(
            P("occ", None, None, "vir"),
            P("occ", None, None, "vir"),
            P("vir", None, None),
            P("vir", None, None),
            P(), P(), P(), P(), P(), P(), P(), P(), P(),
        ),
        out_specs=P("occ", None, None, "vir"),
        check_vma=False,
    )
```

```python
import functools

import jax
import jax.numpy as jnp
from jax import lax
from jax.experimental import pallas as pl
from jax.experimental.pallas import tpu as pltpu
from jax.sharding import PartitionSpec as P

MESH = pl.DeviceIdType.MESH
VMEM_BYTES = 56 * 1024 * 1024


def bits_down(count):
    bits, bit = [], count // 2
    while bit >= 1:
        bits.append(bit)
        bit //= 2
    return bits


def flipped(index, bit):
    return index + bit - 2 * bit * ((index // bit) % 2)


def spread_order(count):
    return sorted(range(1, count), key=lambda step: abs(step - count // 2))


def gather_stages(ref, occ, vir, occ_count, vir_count, send_sem, recv_sem):
    def copies(views, device_id, first):
        return [
            pltpu.make_async_remote_copy(
                src_ref=view, dst_ref=view, send_sem=send_sem.at[first + at], recv_sem=recv_sem.at[first + at],
                device_id=device_id, device_id_type=MESH)
            for at, view in enumerate(views)
        ]

    stages, first = [], 0
    held = [vir]
    for bit in bits_down(vir_count):
        stages.append(copies([ref.at[at, occ] for at in held], (occ, flipped(vir, bit)), first))
        first += len(held)
        held = held + [flipped(at, bit) for at in held]
    held = [occ]
    for bit in bits_down(occ_count):
        stages.append(copies([ref.at[:, at] for at in held], (flipped(occ, bit), vir), first))
        first += len(held)
        held = held + [flipped(at, bit) for at in held]
    return stages


def exchange_kernel(occ_count, vir_count, outward, many_ref, tile_ref, out_ref, every_ref,
                    own_sem, m_send, m_recv, g_send, g_recv):
    occ, vir = lax.axis_index("occ"), lax.axis_index("vir")
    sub, side = every_ref.shape[2], every_ref.shape[3]
    window = out_ref.shape[1 if outward else 0]
    rows = out_ref.shape[2] if outward else many_ref.shape[2]

    barrier = pltpu.get_barrier_semaphore()
    for step in range(1, vir_count):
        peer = (vir + step) % vir_count
        pl.semaphore_signal(barrier, inc=1, device_id=(occ, peer), device_id_type=MESH)
    for bit in bits_down(occ_count):
        pl.semaphore_signal(barrier, inc=1, device_id=(flipped(occ, bit), vir), device_id_type=MESH)

    mine = pltpu.make_async_copy(tile_ref.at[pl.ds(occ * sub, sub)], every_ref.at[vir, occ], own_sem.at[0])
    mine.start()

    def source(peer, j, start):
        if outward:
            return many_ref.at[0, j, pl.ds(peer * rows + start, side), :]
        return many_ref.at[peer, j, pl.ds(start, side), :]

    def target(j, start):
        if outward:
            return out_ref.at[vir, j, pl.ds(start, side), :]
        return out_ref.at[j, pl.ds(vir * rows + start, side), :]

    chunks = [(j, start) for start in range(0, rows, side) for j in range(window)]
    keeps = [
        pltpu.make_async_copy(source(vir, j, start), target(j, start), own_sem.at[1 + at])
        for at, (j, start) in enumerate(chunks)
    ]
    order = spread_order(vir_count)
    moves = []

    def move_next():
        if len(moves) == len(chunks) * len(order):
            return
        j, start = chunks[len(moves) // len(order)]
        for step in order:
            peer, at = (vir + step) % vir_count, len(moves)
            copy = pltpu.make_async_remote_copy(
                src_ref=source(peer, j, start), dst_ref=target(j, start),
                send_sem=m_send.at[at], recv_sem=m_recv.at[at],
                device_id=(occ, peer), device_id_type=MESH)
            copy.start()
            moves.append(copy)

    mine.wait()
    pl.semaphore_wait(barrier, vir_count - 1 + len(bits_down(occ_count)))
    stages = gather_stages(every_ref, occ, vir, occ_count, vir_count, g_send, g_recv)
    wide = len(bits_down(vir_count))
    for at, stage in enumerate(stages):
        for copy in stage:
            copy.start()
        move_next()
        if at == 0:
            for copy in keeps:
                copy.start()
        if at >= wide:
            move_next()
        if at == len(stages) - 1:
            for _ in chunks:
                move_next()
        for copy in stage:
            copy.wait()
    for copy in keeps:
        copy.wait()
    for copy in moves:
        copy.wait()


def exchange(many, tiles, out_shape, occ_count, vir_count, outward):
    stored, side, _ = tiles.shape
    rows, window = (out_shape[2], out_shape[1]) if outward else (many.shape[2], many.shape[1])
    chunks = rows // side * window
    moves, gathers = chunks * (vir_count - 1), vir_count - 1 + occ_count - 1
    every = (vir_count, occ_count, stored // occ_count, side, side)
    out, gathered = pl.pallas_call(
        functools.partial(exchange_kernel, occ_count, vir_count, outward),
        out_shape=(jax.ShapeDtypeStruct(out_shape, jnp.bfloat16), jax.ShapeDtypeStruct(every, jnp.bfloat16)),
        in_specs=[pl.BlockSpec(memory_space=pl.ANY)] * 2,
        out_specs=(pl.BlockSpec(memory_space=pl.ANY),) * 2,
        scratch_shapes=[
            pltpu.SemaphoreType.DMA((1 + chunks,)),
            pltpu.SemaphoreType.DMA((moves,)),
            pltpu.SemaphoreType.DMA((moves,)),
            pltpu.SemaphoreType.DMA((gathers,)),
            pltpu.SemaphoreType.DMA((gathers,)),
        ],
        compiler_params=pltpu.CompilerParams(
            collective_id=0 if outward else 1, has_side_effects=True, vmem_limit_bytes=VMEM_BYTES),
    )(many, tiles)
    return out, gathered.reshape(vir_count * stored, side, side)


def cycle_kernel(screen_ref, used_ref, tx_ref, z_ref, out_ref):
    vir_count, window, rows, block_cols = tx_ref.shape
    side = z_ref.shape[1]
    here, tiles_here = block_cols // side, rows // side
    keep = screen_ref.shape[1]
    tile_count = screen_ref.shape[0] // window
    dest = pl.program_id(0)
    for j in range(window):
        for col in range(here):
            q = j * tile_count + dest * here + col
            picked, weights = [], []
            for m in range(keep):
                u = screen_ref[q, m]
                k, tile = u // tile_count, u % tile_count
                lanes = pl.ds(pl.multiple_of((tile % here) * side, side), side)
                picked.append(tx_ref[tile // here, k, :, lanes])
                weights.append(z_ref[q * keep + m])
            part = jnp.dot(
                jnp.concatenate(picked, axis=1), jnp.concatenate(weights, axis=0),
                preferred_element_type=jnp.float32)
            for a in range(tiles_here):
                span = slice(a * side, (a + 1) * side)
                kept = jnp.where(used_ref[a, q] > 0, part[span], 0.0)
                out_ref[0, j, span, col * side:(col + 1) * side] = kept.astype(jnp.bfloat16)


def cycle_term(cycle_screen, used, moved, all_cycle):
    vir_count, window, rows, block_cols = moved.shape
    return pl.pallas_call(
        cycle_kernel,
        out_shape=jax.ShapeDtypeStruct(moved.shape, jnp.bfloat16),
        grid=(vir_count,),
        in_specs=[
            pl.BlockSpec(memory_space=pltpu.SMEM),
            pl.BlockSpec(memory_space=pltpu.SMEM),
            pl.BlockSpec(moved.shape, lambda d: (0, 0, 0, 0)),
            pl.BlockSpec(all_cycle.shape, lambda d: (0, 0, 0)),
        ],
        out_specs=pl.BlockSpec((1, window, rows, block_cols), lambda d: (d, 0, 0, 0)),
        compiler_params=pltpu.CompilerParams(vmem_limit_bytes=VMEM_BYTES),
    )(cycle_screen, used, moved, all_cycle)


def update_kernel(screen_ref, slot_ref, energy_ref, t_ref, w_ref, row_ref, col_ref, near_ref, cycle_ref, out_ref):
    window = t_ref.shape[1]
    keep = screen_ref.shape[1]
    a = pl.program_id(0)
    weights = jnp.concatenate([w_ref[slot_ref[a * keep + k]] for k in range(keep)], axis=1)
    sums = row_ref[...] + col_ref[...] - energy_ref[0]
    for j in range(window):
        picked = jnp.concatenate([t_ref[0, j, screen_ref[a, k]] for k in range(keep)], axis=0)
        ladder = jnp.dot(weights, picked, preferred_element_type=jnp.float32)
        value = near_ref[0, j].astype(jnp.float32) + ladder + cycle_ref[j].astype(jnp.float32)
        out_ref[0, j] = (value / (sums - energy_ref[1 + j])).astype(jnp.bfloat16)


def update(ladder_screen, tile_slot, energies, amplitudes, all_ladder, energy_a, energy_b, coulomb, cycle):
    _, window, width_all, block_cols = amplitudes.shape
    side = all_ladder.shape[1]
    tile_count = width_all // side
    tiled = amplitudes.reshape(1, window, tile_count, side, block_cols)
    block = pl.BlockSpec((1, window, side, block_cols), lambda a: (0, 0, a, 0))
    smem = pl.BlockSpec(memory_space=pltpu.SMEM)
    return pl.pallas_call(
        update_kernel,
        out_shape=jax.ShapeDtypeStruct(amplitudes.shape, jnp.bfloat16),
        grid=(tile_count,),
        in_specs=[
            smem, smem, smem,
            pl.BlockSpec(tiled.shape, lambda a: (0, 0, 0, 0, 0)),
            pl.BlockSpec(all_ladder.shape, lambda a: (0, 0, 0)),
            pl.BlockSpec((side, 1), lambda a: (a, 0)),
            pl.BlockSpec((1, block_cols), lambda a: (0, 0)),
            block,
            pl.BlockSpec((window, side, block_cols), lambda a: (0, a, 0)),
        ],
        out_specs=block,
        compiler_params=pltpu.CompilerParams(vmem_limit_bytes=VMEM_BYTES),
    )(ladder_screen, tile_slot, energies, tiled, all_ladder, energy_a, energy_b, coulomb, cycle)


def body(
    amplitudes, coulomb, ladder_tiles, cycle_tiles, ladder_screen, tile_slot, cycle_screen,
    cycle_rows, cycle_count, slab_occ, window_occ, occ_energy, vir_energy,
):
    occ_count, vir_count = lax.axis_size("occ"), lax.axis_size("vir")
    slab_rows, window, width_all, block_cols = amplitudes.shape
    stored, side, _ = ladder_tiles.shape
    tile_count = width_all // side
    tiles_here = tile_count // vir_count
    occ, vir = lax.axis_index("occ"), lax.axis_index("vir")

    columns = lax.dynamic_slice_in_dim(cycle_rows, vir * tiles_here, tiles_here, 0)
    counts = lax.dynamic_slice_in_dim(cycle_count, vir * tiles_here, tiles_here, 0)
    listed = jnp.arange(columns.shape[1], dtype=jnp.int32)[None, :] < counts[:, None]
    every_q = jnp.arange(cycle_screen.shape[0], dtype=jnp.int32)
    used = jnp.any((columns[:, :, None] == every_q[None, None, :]) & listed[:, :, None], axis=1).astype(jnp.int32)

    orbital_ids = jnp.arange(occ_energy.shape[0], dtype=jnp.int32)
    wanted = jnp.concatenate([lax.dynamic_slice_in_dim(slab_occ, occ * slab_rows, slab_rows), window_occ])
    energies = jnp.sum(jnp.where(wanted[:, None] == orbital_ids[None, :], occ_energy[None, :], 0.0), axis=1)
    energy_a = vir_energy.reshape(width_all, 1)
    energy_b = lax.dynamic_slice_in_dim(vir_energy, vir * block_cols, block_cols).reshape(1, block_cols)

    moved_shape = (vir_count, window, width_all // vir_count, block_cols)
    moved, all_cycle = exchange(amplitudes, cycle_tiles, moved_shape, occ_count, vir_count, True)
    part = cycle_term(cycle_screen, used, moved, all_cycle)
    cycle, all_ladder = exchange(part, ladder_tiles, amplitudes.shape[1:], occ_count, vir_count, False)
    return update(ladder_screen, tile_slot, energies, amplitudes, all_ladder, energy_a, energy_b, coulomb, cycle)


def solution(mesh):
    return jax.shard_map(
        body,
        mesh=mesh,
        in_specs=(
            P("occ", None, None, "vir"),
            P("occ", None, None, "vir"),
            P("vir", None, None),
            P("vir", None, None),
            P(), P(), P(), P(), P(), P(), P(), P(), P(),
        ),
        out_specs=P("occ", None, None, "vir"),
        check_vma=False,
    )
```

```python
import functools

import jax
import jax.numpy as jnp
from jax import lax
from jax.experimental import pallas as pl
from jax.experimental.pallas import tpu as pltpu
from jax.sharding import PartitionSpec as P

MESH = pl.DeviceIdType.MESH
VMEM_BYTES = 60 * 1024 * 1024


def bits_down(count):
    bits, bit = [], count // 2
    while bit >= 1:
        bits.append(bit)
        bit //= 2
    return bits


def flipped(index, bit):
    return index + bit - 2 * bit * ((index // bit) % 2)


def spread_order(count):
    return sorted(range(1, count), key=lambda step: abs(step - count // 2))


def gather_stages(ref, occ, vir, occ_count, vir_count, send_sem, recv_sem):
    def copies(views, device_id, first):
        return [
            pltpu.make_async_remote_copy(
                src_ref=view, dst_ref=view, send_sem=send_sem.at[first + at], recv_sem=recv_sem.at[first + at],
                device_id=device_id, device_id_type=MESH)
            for at, view in enumerate(views)
        ]

    stages, first = [], 0
    held = [vir]
    for bit in bits_down(vir_count):
        stages.append(copies([ref.at[at, occ] for at in held], (occ, flipped(vir, bit)), first))
        first += len(held)
        held = held + [flipped(at, bit) for at in held]
    held = [occ]
    for bit in bits_down(occ_count):
        stages.append(copies([ref.at[:, at] for at in held], (flipped(occ, bit), vir), first))
        first += len(held)
        held = held + [flipped(at, bit) for at in held]
    return stages


def main_kernel(occ_count, vir_count, lscreen_ref, slot_ref, cscreen_ref, mask_ref, t_ref, w_ref, z_ref,
                cycle_ref, ladder_ref, *scratch):
    groups = 2
    tx, part, scratch = scratch[:groups], scratch[groups:2 * groups], scratch[2 * groups:]
    wall, zall, t_own, lad, picks, own_sem, lad_sem, m_send, m_recv, b_send, b_recv, z_send, z_recv, w_send, w_recv = scratch
    occ, vir = lax.axis_index("occ"), lax.axis_index("vir")
    _, window, tile_count, side, block_cols = t_ref.shape
    sub = wall.shape[2]
    stored = sub * occ_count
    tiles_here, here = tile_count // vir_count, block_cols // side
    depth = tiles_here // groups
    ladder_keep, cycle_keep = lscreen_ref.shape[1], cscreen_ref.shape[1]
    occ_bits = bits_down(occ_count)

    barrier = pltpu.get_barrier_semaphore()
    for step in range(1, vir_count):
        peer = (vir + step) % vir_count
        pl.semaphore_signal(barrier, inc=1, device_id=(occ, peer), device_id_type=MESH)
    for bit in occ_bits:
        pl.semaphore_signal(barrier, inc=1, device_id=(flipped(occ, bit), vir), device_id_type=MESH)

    mine = []
    for at, (src, dst) in enumerate(((z_ref, zall), (w_ref, wall))):
        copy = pltpu.make_async_copy(src.at[pl.ds(occ * sub, sub)], dst.at[vir, occ], own_sem.at[at])
        copy.start()
        mine.append(copy)
    whole = pltpu.make_async_copy(t_ref.at[0], t_own, own_sem.at[2])
    keeps = []

    def keep(src, dst):
        copy = pltpu.make_async_copy(src, dst, own_sem.at[3 + len(keeps)])
        copy.start()
        keeps.append(copy)
        return copy

    order = spread_order(vir_count)
    chunks = [(g, d, j) for g in range(groups) for d in range(depth) for j in range(window)]
    moves = [[] for _ in range(groups)]
    moved = 0

    def move_next():
        nonlocal moved
        if moved == len(chunks):
            return
        g, d, j = chunks[moved]
        place = tx[g].at[vir, j, pl.ds(d * side, side), :]
        for lane, step in enumerate(order):
            peer, at = (vir + step) % vir_count, moved * len(order) + lane
            copy = pltpu.make_async_remote_copy(
                src_ref=t_ref.at[0, j, peer * tiles_here + g * depth + d], dst_ref=place,
                send_sem=m_send.at[at], recv_sem=m_recv.at[at],
                device_id=(occ, peer), device_id_type=MESH)
            copy.start()
            moves[g].append(copy)
        moves[g].append(keep(t_ref.at[0, j, vir * tiles_here + g * depth + d], place))
        moved += 1

    for copy in mine:
        copy.wait()
    pl.semaphore_wait(barrier, vir_count - 1 + len(occ_bits))
    z_stages = gather_stages(zall, occ, vir, occ_count, vir_count, z_send, z_recv)
    w_stages = gather_stages(wall, occ, vir, occ_count, vir_count, w_send, w_recv)
    wide = len(bits_down(vir_count))
    for at, stage in enumerate(z_stages):
        for copy in stage:
            copy.start()
        move_next()
        if at == 0:
            whole.start()
        if at >= wide:
            move_next()
        if at == len(z_stages) - 1:
            for _ in chunks:
                move_next()
        for copy in stage:
            copy.wait()

    def start_w(at):
        for copy in w_stages[at]:
            copy.start()

    def wait_w(at):
        for copy in w_stages[at]:
            copy.wait()

    start_w(0)
    backs = []
    for g in range(groups):
        for copy in moves[g]:
            copy.wait()

        def arrange(source, carry, g=g):
            for k in range(window):
                for col in range(here):
                    picks[k * tile_count + source * here + col] = tx[g][source, k, :, col * side:(col + 1) * side]
            return carry

        lax.fori_loop(0, vir_count, arrange, 0)

        def products(index, carry, g=g):
            j, dest = index // vir_count, index % vir_count
            for col in range(here):
                q = j * tile_count + dest * here + col
                picked, weights = [], []
                for m in range(cycle_keep):
                    picked.append(picks[cscreen_ref[q, m]])
                    slot = q * cycle_keep + m
                    weights.append(zall[slot // stored, (slot % stored) // sub, slot % sub])
                total = jnp.dot(
                    jnp.concatenate(picked, axis=1), jnp.concatenate(weights, axis=0),
                    preferred_element_type=jnp.float32)
                for d in range(depth):
                    kept = total[d * side:(d + 1) * side] * mask_ref[g * depth + d, q]
                    part[g][dest, j, d * side:(d + 1) * side, col * side:(col + 1) * side] = kept.astype(jnp.bfloat16)
            return carry

        lax.fori_loop(0, window * vir_count, products, 0)
        place = cycle_ref.at[:, pl.ds((vir * tiles_here + g * depth) * side, depth * side), :]
        for lane, step in enumerate(order):
            peer, at = (vir + step) % vir_count, g * len(order) + lane
            copy = pltpu.make_async_remote_copy(
                src_ref=part[g].at[peer], dst_ref=place, send_sem=b_send.at[at], recv_sem=b_recv.at[at],
                device_id=(occ, peer), device_id_type=MESH)
            copy.start()
            backs.append(copy)
        backs.append(keep(part[g].at[vir], place))
        wait_w(g)
        start_w(g + 1)

    for at in range(groups, len(w_stages)):
        wait_w(at)
        if at + 1 < len(w_stages):
            start_w(at + 1)
    whole.wait()

    batch = lad.shape[1]
    written = []
    for block in range(tile_count // batch):
        if block >= 2:
            written[block - 2].wait()

        def ladder_tile(index, carry, block=block):
            a = block * batch + index
            weights = []
            for k in range(ladder_keep):
                at = a * ladder_keep + k
                weights.append(wall[slot_ref[0, at], slot_ref[1, at], slot_ref[2, at]])
            weights = jnp.concatenate(weights, axis=1)
            for j in range(window):
                picked = jnp.concatenate([t_own[j, lscreen_ref[a, k]] for k in range(ladder_keep)], axis=0)
                lad[block % 2, index, j] = jnp.dot(weights, picked, preferred_element_type=jnp.float32)
            return carry

        lax.fori_loop(0, batch, ladder_tile, 0)
        copy = pltpu.make_async_copy(
            lad.at[block % 2], ladder_ref.at[pl.ds(block * batch, batch)], lad_sem.at[block])
        copy.start()
        written.append(copy)
    for copy in written[-2:]:
        copy.wait()
    for copy in backs:
        copy.wait()


def terms(ladder_screen, tile_slot, cycle_screen, used, tiled, ladder_tiles, cycle_tiles, occ_count, vir_count):
    _, window, tile_count, side, block_cols = tiled.shape
    stored = ladder_tiles.shape[0]
    groups, batch = 2, 8
    sub = stored // occ_count
    slots = jnp.stack([tile_slot // stored, (tile_slot % stored) // sub, tile_slot % sub])
    mask = jnp.broadcast_to(used.astype(jnp.float32)[:, :, None, None], used.shape + (1, side))
    tiles_here = tile_count // vir_count
    moves, gathers = tiles_here * window * (vir_count - 1), vir_count - 1 + occ_count - 1
    backs = groups * (vir_count - 1)
    group_shape = (vir_count, window, tiles_here // groups * side, block_cols)
    every = (vir_count, occ_count, stored // occ_count, side, side)
    smem, anywhere = pl.BlockSpec(memory_space=pltpu.SMEM), pl.BlockSpec(memory_space=pl.ANY)
    sems = [3 + tiles_here * window + groups, tile_count // batch,
            moves, moves, backs, backs, gathers, gathers, gathers, gathers]
    return pl.pallas_call(
        functools.partial(main_kernel, occ_count, vir_count),
        out_shape=(
            jax.ShapeDtypeStruct((window, tile_count * side, block_cols), jnp.bfloat16),
            jax.ShapeDtypeStruct((tile_count, window, side, block_cols), jnp.float32),
        ),
        in_specs=[smem] * 3 + [pl.BlockSpec(memory_space=pltpu.VMEM)] + [anywhere] * 3,
        out_specs=(anywhere,) * 2,
        scratch_shapes=[pltpu.VMEM(group_shape, jnp.bfloat16)] * (2 * groups) + [
            pltpu.VMEM(every, jnp.bfloat16),
            pltpu.VMEM(every, jnp.bfloat16),
            pltpu.VMEM((window, tile_count, side, block_cols), jnp.bfloat16),
            pltpu.VMEM((2, batch, window, side, block_cols), jnp.float32),
            pltpu.VMEM((window * tile_count, tiles_here // groups * side, side), jnp.bfloat16),
        ] + [pltpu.SemaphoreType.DMA((count,)) for count in sems],
        compiler_params=pltpu.CompilerParams(
            collective_id=0, has_side_effects=True, vmem_limit_bytes=VMEM_BYTES),
    )(ladder_screen, slots, cycle_screen, mask, tiled, ladder_tiles, cycle_tiles)


def update_kernel(energy_ref, row_ref, col_ref, near_ref, cycle_ref, ladder_ref, out_ref):
    tiles, window, side, _ = ladder_ref.shape
    for at in range(tiles):
        span = slice(at * side, (at + 1) * side)
        sums = row_ref[span] + col_ref[...] - energy_ref[0]
        for j in range(window):
            value = near_ref[0, j, span].astype(jnp.float32) + ladder_ref[at, j] + cycle_ref[j, span].astype(jnp.float32)
            out_ref[0, j, span] = (value / (sums - energy_ref[1 + j])).astype(jnp.bfloat16)


def update(energies, energy_a, energy_b, coulomb, cycle, ladder):
    tile_count, window, side, block_cols = ladder.shape
    tiles = 2
    block = pl.BlockSpec((1, window, tiles * side, block_cols), lambda a: (0, 0, a, 0))
    return pl.pallas_call(
        update_kernel,
        out_shape=jax.ShapeDtypeStruct(coulomb.shape, jnp.bfloat16),
        grid=(tile_count // tiles,),
        in_specs=[
            pl.BlockSpec(memory_space=pltpu.SMEM),
            pl.BlockSpec((tiles * side, 1), lambda a: (a, 0)),
            pl.BlockSpec((1, block_cols), lambda a: (0, 0)),
            block,
            pl.BlockSpec((window, tiles * side, block_cols), lambda a: (0, a, 0)),
            pl.BlockSpec((tiles, window, side, block_cols), lambda a: (a, 0, 0, 0)),
        ],
        out_specs=block,
        compiler_params=pltpu.CompilerParams(vmem_limit_bytes=VMEM_BYTES),
    )(energies, energy_a, energy_b, coulomb, cycle, ladder)


def body(
    amplitudes, coulomb, ladder_tiles, cycle_tiles, ladder_screen, tile_slot, cycle_screen,
    cycle_rows, cycle_count, slab_occ, window_occ, occ_energy, vir_energy,
):
    occ_count, vir_count = lax.axis_size("occ"), lax.axis_size("vir")
    slab_rows, window, width_all, block_cols = amplitudes.shape
    stored, side, _ = ladder_tiles.shape
    tile_count = width_all // side
    tiles_here = tile_count // vir_count
    occ, vir = lax.axis_index("occ"), lax.axis_index("vir")

    columns = lax.dynamic_slice_in_dim(cycle_rows, vir * tiles_here, tiles_here, 0)
    counts = lax.dynamic_slice_in_dim(cycle_count, vir * tiles_here, tiles_here, 0)
    listed = jnp.arange(columns.shape[1], dtype=jnp.int32)[None, :] < counts[:, None]
    every_q = jnp.arange(cycle_screen.shape[0], dtype=jnp.int32)
    used = jnp.any((columns[:, :, None] == every_q[None, None, :]) & listed[:, :, None], axis=1).astype(jnp.int32)

    orbital_ids = jnp.arange(occ_energy.shape[0], dtype=jnp.int32)
    wanted = jnp.concatenate([lax.dynamic_slice_in_dim(slab_occ, occ * slab_rows, slab_rows), window_occ])
    energies = jnp.sum(jnp.where(wanted[:, None] == orbital_ids[None, :], occ_energy[None, :], 0.0), axis=1)
    energy_a = vir_energy.reshape(width_all, 1)
    energy_b = lax.dynamic_slice_in_dim(vir_energy, vir * block_cols, block_cols).reshape(1, block_cols)

    tiled = amplitudes.reshape(slab_rows, window, tile_count, side, block_cols)
    cycle, ladder = terms(
        ladder_screen, tile_slot, cycle_screen, used, tiled, ladder_tiles, cycle_tiles, occ_count, vir_count)
    return update(energies, energy_a, energy_b, coulomb, cycle, ladder)


def solution(mesh):
    return jax.shard_map(
        body,
        mesh=mesh,
        in_specs=(
            P("occ", None, None, "vir"),
            P("occ", None, None, "vir"),
            P("vir", None, None),
            P("vir", None, None),
            P(), P(), P(), P(), P(), P(), P(), P(), P(),
        ),
        out_specs=P("occ", None, None, "vir"),
        check_vma=False,
    )
```

```python
import functools

import jax
import jax.numpy as jnp
from jax import lax
from jax.experimental import pallas as pl
from jax.experimental.pallas import tpu as pltpu
from jax.sharding import PartitionSpec as P

MESH = pl.DeviceIdType.MESH
VMEM_BYTES = 60 * 1024 * 1024


def bits_down(count):
    bits, bit = [], count // 2
    while bit >= 1:
        bits.append(bit)
        bit //= 2
    return bits


def flipped(index, bit):
    return index + bit - 2 * bit * ((index // bit) % 2)


def spread_order(count):
    return sorted(range(1, count), key=lambda step: abs(step - count // 2))


def gather_stages(ref, occ, vir, occ_count, vir_count, send_sem, recv_sem):
    def copies(views, device_id, first):
        return [
            pltpu.make_async_remote_copy(
                src_ref=view, dst_ref=view, send_sem=send_sem.at[first + at], recv_sem=recv_sem.at[first + at],
                device_id=device_id, device_id_type=MESH)
            for at, view in enumerate(views)
        ]

    stages, first = [], 0
    held = [vir]
    for bit in bits_down(vir_count):
        stages.append(copies([ref.at[at, occ] for at in held], (occ, flipped(vir, bit)), first))
        first += len(held)
        held = held + [flipped(at, bit) for at in held]
    held = [occ]
    for bit in bits_down(occ_count):
        stages.append(copies([ref.at[:, at] for at in held], (flipped(occ, bit), vir), first))
        first += len(held)
        held = held + [flipped(at, bit) for at in held]
    return stages


def main_kernel(occ_count, vir_count, lscreen_ref, slot_ref, cscreen_ref, mask_ref, t_ref, w_ref, z_ref,
                cycle_ref, ladder_ref, *scratch):
    groups = 2
    tx, part, scratch = scratch[:groups], scratch[groups:2 * groups], scratch[2 * groups:]
    wall, zall, t_own, lad, picks, own_sem, lad_sem, m_send, m_recv, b_send, b_recv, z_send, z_recv, w_send, w_recv = scratch
    occ, vir = lax.axis_index("occ"), lax.axis_index("vir")
    _, window, tile_count, side, block_cols = t_ref.shape
    sub = wall.shape[2]
    stored = sub * occ_count
    tiles_here, here = tile_count // vir_count, block_cols // side
    depth = tiles_here // groups
    ladder_keep, cycle_keep = lscreen_ref.shape[1], cscreen_ref.shape[1]
    occ_bits = bits_down(occ_count)

    barrier = pltpu.get_barrier_semaphore()
    for step in range(1, vir_count):
        peer = (vir + step) % vir_count
        pl.semaphore_signal(barrier, inc=1, device_id=(occ, peer), device_id_type=MESH)
    for bit in occ_bits:
        pl.semaphore_signal(barrier, inc=1, device_id=(flipped(occ, bit), vir), device_id_type=MESH)

    mine = []
    for at, (src, dst) in enumerate(((z_ref, zall), (w_ref, wall))):
        copy = pltpu.make_async_copy(src.at[pl.ds(occ * sub, sub)], dst.at[vir, occ], own_sem.at[at])
        copy.start()
        mine.append(copy)
    whole = pltpu.make_async_copy(t_ref.at[0], t_own, own_sem.at[2])
    keeps = []

    def keep(src, dst):
        copy = pltpu.make_async_copy(src, dst, own_sem.at[3 + len(keeps)])
        copy.start()
        keeps.append(copy)
        return copy

    order = spread_order(vir_count)
    chunks = [(g, d, j) for g in range(groups) for d in range(depth) for j in range(window)]
    moves = [[] for _ in range(groups)]
    moved = 0

    def move_next():
        nonlocal moved
        if moved == len(chunks):
            return
        g, d, j = chunks[moved]
        place = tx[g].at[vir, j, pl.ds(d * side, side), :]
        for lane, step in enumerate(order):
            peer, at = (vir + step) % vir_count, moved * len(order) + lane
            copy = pltpu.make_async_remote_copy(
                src_ref=t_ref.at[0, j, peer * tiles_here + g * depth + d], dst_ref=place,
                send_sem=m_send.at[at], recv_sem=m_recv.at[at],
                device_id=(occ, peer), device_id_type=MESH)
            copy.start()
            moves[g].append(copy)
        moves[g].append(keep(t_ref.at[0, j, vir * tiles_here + g * depth + d], place))
        moved += 1

    for copy in mine:
        copy.wait()
    pl.semaphore_wait(barrier, vir_count - 1 + len(occ_bits))
    z_stages = gather_stages(zall, occ, vir, occ_count, vir_count, z_send, z_recv)
    w_stages = gather_stages(wall, occ, vir, occ_count, vir_count, w_send, w_recv)
    wide = len(bits_down(vir_count))
    for at, stage in enumerate(z_stages):
        stage = stage + (w_stages[at] if at < wide else [])
        for copy in stage:
            copy.start()
        move_next()
        if at == 0:
            whole.start()
        if at >= wide:
            move_next()
        if at == len(z_stages) - 1:
            for _ in chunks:
                move_next()
        for copy in stage:
            copy.wait()

    def start_w(at):
        for copy in w_stages[at]:
            copy.start()

    def wait_w(at):
        for copy in w_stages[at]:
            copy.wait()

    start_w(wide)
    backs = []
    for g in range(groups):
        for copy in moves[g]:
            copy.wait()

        def arrange(source, carry, g=g):
            for k in range(window):
                for col in range(here):
                    picks[k * tile_count + source * here + col] = tx[g][source, k, :, col * side:(col + 1) * side]
            return carry

        lax.fori_loop(0, vir_count, arrange, 0)

        def products(index, carry, g=g):
            j, dest = index // vir_count, index % vir_count
            for col in range(here):
                q = j * tile_count + dest * here + col
                picked, weights = [], []
                for m in range(cycle_keep):
                    picked.append(picks[cscreen_ref[q, m]])
                    slot = q * cycle_keep + m
                    weights.append(zall[slot // stored, (slot % stored) // sub, slot % sub])
                total = jnp.dot(
                    jnp.concatenate(picked, axis=1), jnp.concatenate(weights, axis=0),
                    preferred_element_type=jnp.float32)
                for d in range(depth):
                    kept = total[d * side:(d + 1) * side] * mask_ref[g * depth + d, q]
                    part[g][dest, j, d * side:(d + 1) * side, col * side:(col + 1) * side] = kept.astype(jnp.bfloat16)
            return carry

        lax.fori_loop(0, window * vir_count, products, 0)
        place = cycle_ref.at[:, pl.ds((vir * tiles_here + g * depth) * side, depth * side), :]
        for lane, step in enumerate(order):
            peer, at = (vir + step) % vir_count, g * len(order) + lane
            copy = pltpu.make_async_remote_copy(
                src_ref=part[g].at[peer], dst_ref=place, send_sem=b_send.at[at], recv_sem=b_recv.at[at],
                device_id=(occ, peer), device_id_type=MESH)
            copy.start()
            backs.append(copy)
        backs.append(keep(part[g].at[vir], place))
        if wide + g < len(w_stages):
            wait_w(wide + g)
        if wide + g + 1 < len(w_stages):
            start_w(wide + g + 1)

    for at in range(wide + groups, len(w_stages)):
        wait_w(at)
        if at + 1 < len(w_stages):
            start_w(at + 1)
    whole.wait()

    batch = lad.shape[1]
    written = []
    for block in range(tile_count // batch):
        if block >= 2:
            written[block - 2].wait()

        def ladder_tile(index, carry, block=block):
            a = block * batch + index
            weights = []
            for k in range(ladder_keep):
                at = a * ladder_keep + k
                weights.append(wall[slot_ref[0, at], slot_ref[1, at], slot_ref[2, at]])
            weights = jnp.concatenate(weights, axis=1)
            for j in range(window):
                picked = jnp.concatenate([t_own[j, lscreen_ref[a, k]] for k in range(ladder_keep)], axis=0)
                lad[block % 2, index, j] = jnp.dot(weights, picked, preferred_element_type=jnp.float32)
            return carry

        lax.fori_loop(0, batch, ladder_tile, 0)
        copy = pltpu.make_async_copy(
            lad.at[block % 2], ladder_ref.at[pl.ds(block * batch, batch)], lad_sem.at[block])
        copy.start()
        written.append(copy)
    for copy in written[-2:]:
        copy.wait()
    for copy in backs:
        copy.wait()


def terms(ladder_screen, tile_slot, cycle_screen, used, tiled, ladder_tiles, cycle_tiles, occ_count, vir_count):
    _, window, tile_count, side, block_cols = tiled.shape
    stored = ladder_tiles.shape[0]
    groups, batch = 2, 8
    sub = stored // occ_count
    slots = jnp.stack([tile_slot // stored, (tile_slot % stored) // sub, tile_slot % sub])
    mask = jnp.broadcast_to(used.astype(jnp.float32)[:, :, None, None], used.shape + (1, side))
    tiles_here = tile_count // vir_count
    moves, gathers = tiles_here * window * (vir_count - 1), vir_count - 1 + occ_count - 1
    backs = groups * (vir_count - 1)
    group_shape = (vir_count, window, tiles_here // groups * side, block_cols)
    every = (vir_count, occ_count, stored // occ_count, side, side)
    smem, anywhere = pl.BlockSpec(memory_space=pltpu.SMEM), pl.BlockSpec(memory_space=pl.ANY)
    sems = [3 + tiles_here * window + groups, tile_count // batch,
            moves, moves, backs, backs, gathers, gathers, gathers, gathers]
    return pl.pallas_call(
        functools.partial(main_kernel, occ_count, vir_count),
        out_shape=(
            jax.ShapeDtypeStruct((window, tile_count * side, block_cols), jnp.bfloat16),
            jax.ShapeDtypeStruct((tile_count, window, side, block_cols), jnp.float32),
        ),
        in_specs=[smem] * 3 + [pl.BlockSpec(memory_space=pltpu.VMEM)] + [anywhere] * 3,
        out_specs=(anywhere,) * 2,
        scratch_shapes=[pltpu.VMEM(group_shape, jnp.bfloat16)] * (2 * groups) + [
            pltpu.VMEM(every, jnp.bfloat16),
            pltpu.VMEM(every, jnp.bfloat16),
            pltpu.VMEM((window, tile_count, side, block_cols), jnp.bfloat16),
            pltpu.VMEM((2, batch, window, side, block_cols), jnp.float32),
            pltpu.VMEM((window * tile_count, tiles_here // groups * side, side), jnp.bfloat16),
        ] + [pltpu.SemaphoreType.DMA((count,)) for count in sems],
        compiler_params=pltpu.CompilerParams(
            collective_id=0, has_side_effects=True, vmem_limit_bytes=VMEM_BYTES),
    )(ladder_screen, slots, cycle_screen, mask, tiled, ladder_tiles, cycle_tiles)


def update_kernel(energy_ref, row_ref, col_ref, near_ref, cycle_ref, ladder_ref, out_ref):
    tiles, window, side, _ = ladder_ref.shape
    for at in range(tiles):
        span = slice(at * side, (at + 1) * side)
        sums = row_ref[span] + col_ref[...] - energy_ref[0]
        for j in range(window):
            value = near_ref[0, j, span].astype(jnp.float32) + ladder_ref[at, j] + cycle_ref[j, span].astype(jnp.float32)
            out_ref[0, j, span] = (value / (sums - energy_ref[1 + j])).astype(jnp.bfloat16)


def update(energies, energy_a, energy_b, coulomb, cycle, ladder):
    tile_count, window, side, block_cols = ladder.shape
    tiles = 2
    block = pl.BlockSpec((1, window, tiles * side, block_cols), lambda a: (0, 0, a, 0))
    return pl.pallas_call(
        update_kernel,
        out_shape=jax.ShapeDtypeStruct(coulomb.shape, jnp.bfloat16),
        grid=(tile_count // tiles,),
        in_specs=[
            pl.BlockSpec(memory_space=pltpu.SMEM),
            pl.BlockSpec((tiles * side, 1), lambda a: (a, 0)),
            pl.BlockSpec((1, block_cols), lambda a: (0, 0)),
            block,
            pl.BlockSpec((window, tiles * side, block_cols), lambda a: (0, a, 0)),
            pl.BlockSpec((tiles, window, side, block_cols), lambda a: (a, 0, 0, 0)),
        ],
        out_specs=block,
        compiler_params=pltpu.CompilerParams(vmem_limit_bytes=VMEM_BYTES),
    )(energies, energy_a, energy_b, coulomb, cycle, ladder)


def body(
    amplitudes, coulomb, ladder_tiles, cycle_tiles, ladder_screen, tile_slot, cycle_screen,
    cycle_rows, cycle_count, slab_occ, window_occ, occ_energy, vir_energy,
):
    occ_count, vir_count = lax.axis_size("occ"), lax.axis_size("vir")
    slab_rows, window, width_all, block_cols = amplitudes.shape
    stored, side, _ = ladder_tiles.shape
    tile_count = width_all // side
    tiles_here = tile_count // vir_count
    occ, vir = lax.axis_index("occ"), lax.axis_index("vir")

    columns = lax.dynamic_slice_in_dim(cycle_rows, vir * tiles_here, tiles_here, 0)
    counts = lax.dynamic_slice_in_dim(cycle_count, vir * tiles_here, tiles_here, 0)
    listed = jnp.arange(columns.shape[1], dtype=jnp.int32)[None, :] < counts[:, None]
    every_q = jnp.arange(cycle_screen.shape[0], dtype=jnp.int32)
    used = jnp.any((columns[:, :, None] == every_q[None, None, :]) & listed[:, :, None], axis=1).astype(jnp.int32)

    orbital_ids = jnp.arange(occ_energy.shape[0], dtype=jnp.int32)
    wanted = jnp.concatenate([lax.dynamic_slice_in_dim(slab_occ, occ * slab_rows, slab_rows), window_occ])
    energies = jnp.sum(jnp.where(wanted[:, None] == orbital_ids[None, :], occ_energy[None, :], 0.0), axis=1)
    energy_a = vir_energy.reshape(width_all, 1)
    energy_b = lax.dynamic_slice_in_dim(vir_energy, vir * block_cols, block_cols).reshape(1, block_cols)

    tiled = amplitudes.reshape(slab_rows, window, tile_count, side, block_cols)
    cycle, ladder = terms(
        ladder_screen, tile_slot, cycle_screen, used, tiled, ladder_tiles, cycle_tiles, occ_count, vir_count)
    return update(energies, energy_a, energy_b, coulomb, cycle, ladder)


def solution(mesh):
    return jax.shard_map(
        body,
        mesh=mesh,
        in_specs=(
            P("occ", None, None, "vir"),
            P("occ", None, None, "vir"),
            P("vir", None, None),
            P("vir", None, None),
            P(), P(), P(), P(), P(), P(), P(), P(), P(),
        ),
        out_specs=P("occ", None, None, "vir"),
        check_vma=False,
    )
```
